32 devices in a mesh: dom: 32 (over z, y, x, core).
Axes of the slice: x: 2, y: 2, z: 4, core: 2. Of those that a mesh axis runs over, the one named last changes fastest.
Arguments:
- features: bfloat16 [36864, 128], P('dom'), may hold values from -6 to 6
- targets: bfloat16 [36864, 128], P('dom'), may hold values from -6 to 6
- first_weight: bfloat16 [128, 128], replicated, may hold values from -0.5 to 0.5
- second_weight: bfloat16 [128, 128], replicated, may hold values from -0.5 to 0.5
- local_bonds: bfloat16 [36864, 1152], P('dom'), may hold values from -0.4375 to 0.4375
- halo_bonds: bfloat16 [36864, 512], P('dom'), may hold values from -0.4375 to 0.4375
- tile_mask: int32 [576, 18], P('dom'), may hold values 0 or 1
- send_rows: int32 [128, 128], P('dom'), may hold values from 0 to 1151
Outputs:
- prediction: bfloat16 [36864, 128], P('dom')
- grad_first: float32 [128, 128], replicated
- grad_second: float32 [128, 128], replicated
The draws below stay inside these ranges and needn't reach their ends.
Inputs may be any that keep to these rules, and one draw needn't show every extreme that they name: `tile_mask`: tile presence flags. `send_rows`: local atom numbers of the sending partition; repeats allowed.
All inputs are finite; a program needn't handle non-finite values. No bound on the sum of `tile_mask` on one device may be relied on, other than what follows from the above.
Results may differ from the reference program's by a relative error of at most 0.004.
The reference program's roundings to bfloat16 on the way count: a program that leaves them out, or rounds other values in their place, can miss the bound.
Values may be sent and summed in bfloat16 or wider, within the bound.
No kernel may reach another device: no remote copies, remote signals or barrier semaphores. Data moves between devices by JAX's collectives and lax.ppermute only.
A program may use at most 64 MiB of HBM per device.

```python
import math
import jax
import jax.numpy as jnp
from jax import lax

H = 128
NODE_DEV = 1152
HALO = 128
ROUNDS = 4
TILES_DEV = 18
NODES = 36864
N_DOM = 32


def with_ends(entries, key, low, top_value):
    longest = entries.shape.index(max(entries.shape))
    spots = []
    for shift in (0, 1):
        where = [jax.random.randint(jax.random.fold_in(key, axis), (), 0, length) for axis, length in enumerate(entries.shape)]
        where[longest] = (where[longest] + shift) % entries.shape[longest]
        spots.append(tuple(where))
    return entries.at[spots[0]].set(low).at[spots[1]].set(top_value)


def block_levels(key, shape, split, smallest, high):
    loudness, own = 1.0, jax.random.fold_in(key, 6)
    for dim, parts in split:
        heights = jnp.exp(jax.random.uniform(jax.random.fold_in(own, dim), (parts,), jnp.float32, smallest / len(split), high / len(split)))
        loudness = loudness * jnp.repeat(heights, shape[dim] // parts).reshape([-1 if axis == dim else 1 for axis in range(len(shape))])
    return loudness


def scatter_about(own_key, extent, spread, most, cuts=(), kind=jnp.bfloat16):
    loudness = block_levels(own_key, extent, cuts, -0.22, 0.18) if cuts else 1.0
    result = jax.random.normal(own_key, extent, jnp.float32) * spread * loudness
    return jnp.minimum(jnp.maximum(result, -most), most).astype(kind)


def setup_inputs(seed: int = 0) -> dict:
    key_list = jax.random.split(jax.random.key(seed), 9)
    return {
        "features": scatter_about(key_list[0], (NODES, H), 1.0, 6.0, ((0, 32),)),
        "targets": scatter_about(key_list[1], (NODES, H), 1.0, 6.0, ((0, 32),)),
        "first_weight": scatter_about(key_list[2], (H, H), H ** -0.5, 0.5),
        "second_weight": scatter_about(key_list[3], (H, H), H ** -0.5, 0.5),
        "local_bonds": scatter_about(key_list[4], (NODES, NODE_DEV), ((NODE_DEV // 2 + ROUNDS * HALO) ** -0.5), 0.4375, ((0, 32),)),
        "halo_bonds": scatter_about(key_list[5], (NODES, ROUNDS * HALO), ((NODE_DEV // 2 + ROUNDS * HALO) ** -0.5), 0.4375, ((0, 32),)),
        "tile_mask": with_ends((jax.random.randint(key_list[6], (N_DOM * TILES_DEV, TILES_DEV), 0, 2) < 1).astype(jnp.int32), jax.random.fold_in(key_list[6], 1), 0, 1),
        "send_rows": with_ends(jax.random.randint(key_list[7], (N_DOM * ROUNDS, HALO), 0, NODE_DEV), jax.random.fold_in(key_list[7], 1), 0, NODE_DEV - 1).astype(jnp.int32),
    }


def expand_mask(mask):
    return jnp.repeat(jnp.repeat(mask, 64, axis=0), 64, axis=1).astype(jnp.bfloat16)

def reference(features, targets, first_weight, second_weight, local_bonds, halo_bonds, tile_mask, send_rows):
    bond_all = local_bonds.reshape(N_DOM, NODE_DEV, NODE_DEV)
    mask_all = tile_mask.reshape(N_DOM, TILES_DEV, TILES_DEV)
    halo_all = halo_bonds.reshape(N_DOM, NODE_DEV, ROUNDS * HALO)
    sends = send_rows.reshape(N_DOM, ROUNDS, HALO)
    devices = jnp.arange(N_DOM, dtype=jnp.int32)

    def pick_rows(table, index):
        return table[index]

    def add_rows(table, index, pieces):
        return table.at[index].add(pieces)

    def halo_of(rows):
        pieces = []
        for turn in range(ROUNDS):
            picked = jax.vmap(pick_rows)(rows, sends[:, turn])
            pieces.append(picked[jnp.bitwise_xor(devices, 1 << turn)])
        return jnp.concatenate(pieces, axis=1)

    def local_sum(items):
        bonds, mask, halo_b, rows, halo_rows = items
        tiles = bonds * expand_mask(mask)
        return jnp.dot(tiles, rows, preferred_element_type=jnp.float32) + jnp.dot(halo_b, halo_rows, preferred_element_type=jnp.float32)

    def local_back(items):
        bonds, mask, halo_b, cotan = items
        tiles = bonds * expand_mask(mask)
        return (jnp.dot(tiles.T, cotan, preferred_element_type=jnp.float32), jnp.dot(halo_b.T, cotan, preferred_element_type=jnp.float32))
    feats = features.reshape(N_DOM, NODE_DEV, H)
    first_agg = lax.map(local_sum, (bond_all, mask_all, halo_all, feats, halo_of(feats))).astype(jnp.bfloat16)
    flat_first = first_agg.reshape(NODES, H)
    first_pre = jnp.dot(flat_first, first_weight, preferred_element_type=jnp.float32)
    hidden = (features.astype(jnp.float32) + jax.nn.silu(first_pre)).astype(jnp.bfloat16)
    hid3 = hidden.reshape(N_DOM, NODE_DEV, H)
    second_agg = lax.map(local_sum, (bond_all, mask_all, halo_all, hid3, halo_of(hid3))).astype(jnp.bfloat16)
    flat_second = second_agg.reshape(NODES, H)
    output = hidden.astype(jnp.float32) + jnp.dot(flat_second, second_weight, preferred_element_type=jnp.float32)
    prediction = output.astype(jnp.bfloat16)
    error = (output - targets.astype(jnp.float32)) * (1.0 / math.sqrt(NODES))
    error_b = error.astype(jnp.bfloat16)
    grad_second = jnp.dot(flat_second.T, error_b, preferred_element_type=jnp.float32)
    agg_cot = jnp.dot(error_b, second_weight.T, preferred_element_type=jnp.float32).astype(jnp.bfloat16)
    local_cot, halo_cot = lax.map(local_back, (bond_all, mask_all, halo_all, agg_cot.reshape(N_DOM, NODE_DEV, H)))
    total = jnp.zeros((N_DOM, NODE_DEV, H), jnp.float32)
    for turn in range(ROUNDS):
        block = halo_cot[:, turn * HALO:(turn + 1) * HALO][jnp.bitwise_xor(devices, 1 << turn)]
        total = jax.vmap(add_rows)(total, sends[:, turn], block)
    hidden_cot = error + (local_cot + total).reshape(NODES, H)
    sigm = jax.nn.sigmoid(first_pre)
    pre_cot = (hidden_cot * sigm * (1.0 + first_pre * (1.0 - sigm))).astype(jnp.bfloat16)
    grad_first = jnp.dot(flat_first.T, pre_cot, preferred_element_type=jnp.float32)
    return (prediction, grad_first, grad_second)
```

```python
import functools
import math

import jax
import jax.numpy as jnp
from jax import lax
from jax.experimental import pallas as pl
from jax.experimental.pallas import tpu as pltpu
from jax.sharding import PartitionSpec as P

TILE = 64
PARAMS = pltpu.CompilerParams(vmem_limit_bytes=16 * 2**20)


def swapped(value, mask):
    pairs = [(source, source ^ mask) for source in range(lax.axis_size("dom"))]
    return lax.ppermute(value, "dom", pairs)


def dot(left, right):
    return jnp.dot(left, right, preferred_element_type=jnp.float32)


def dot_rows(left, right):
    return lax.dot_general(
        left, right, (((0,), (0,)), ((), ())), preferred_element_type=jnp.float32
    )


def dot_last(left, right):
    return lax.dot_general(
        left, right, (((1,), (1,)), ((), ())), preferred_element_type=jnp.float32
    )


def call(body, outs, *args):
    args = [pltpu.with_memory_space_constraint(arg, pltpu.VMEM) for arg in args]
    return pl.pallas_call(
        body,
        out_shape=[pltpu.VMEM(shape, dtype) for shape, dtype in outs],
        in_specs=[pl.BlockSpec(memory_space=pltpu.VMEM)] * len(args),
        out_specs=[pl.BlockSpec(memory_space=pltpu.VMEM)] * len(outs),
        compiler_params=PARAMS,
    )(*args)


def pick_kernel(features, send_rows, picker, *picked):
    rounds, width = send_rows.shape
    atoms = features.shape[0]
    rows = jnp.concatenate(
        [send_rows[...], jnp.zeros((8 - rounds, width), jnp.int32)], axis=0
    ).T
    column = lax.broadcasted_iota(jnp.int32, (width, atoms), 1)
    for turn in range(rounds):
        chosen = (rows[:, turn : turn + 1] == column).astype(jnp.float32).astype(jnp.bfloat16)
        picker[turn * width : (turn + 1) * width, :] = chosen
        picked[turn][...] = dot(chosen, features[...]).astype(jnp.bfloat16)


def inner_kernel(local_bonds, tile_mask, features, bonds, inner):
    tiles = tile_mask.shape[0]
    atoms = local_bonds.shape[0]
    spread = (
        lax.broadcasted_iota(jnp.int32, (tiles, atoms), 1) // TILE
        == lax.broadcasted_iota(jnp.int32, (tiles, atoms), 0)
    ).astype(jnp.float32).astype(jnp.bfloat16)
    wide = dot(tile_mask[...].astype(jnp.float32).astype(jnp.bfloat16), spread).astype(jnp.bfloat16)
    for tile in range(tiles):
        rows = slice(tile * TILE, (tile + 1) * TILE)
        bonds[rows, :] = local_bonds[rows, :] * wide[tile : tile + 1, :]
    inner[...] = dot(bonds[...], features[...])


def first_kernel(inner, halo_bonds, picker, halo0, halo1, halo2, halo3, agg, *picked):
    width = halo0.shape[0]
    total = inner[...]
    for turn, halo in enumerate((halo0, halo1, halo2, halo3)):
        total += dot(halo_bonds[:, turn * width : (turn + 1) * width], halo[...])
    agg[...] = total.astype(jnp.bfloat16)
    for turn in range(len(picked)):
        rows = picker[turn * width : (turn + 1) * width, :]
        picked[turn][...] = dot(rows, agg[...]).astype(jnp.bfloat16)


def hidden_kernel(agg, first_weight, features, bonds, hidden, slope, inner):
    pre = dot(agg[...], first_weight[...])
    sigm = jax.nn.sigmoid(pre)
    slope[...] = sigm * (1.0 + pre * (1.0 - sigm))
    hidden[...] = (features[...].astype(jnp.float32) + pre * sigm).astype(jnp.bfloat16)
    inner[...] = dot(bonds[...], hidden[...])


def back_kernel(
    scale,
    inner,
    hidden,
    slope,
    agg,
    bonds,
    halo_bonds,
    targets,
    first_weight,
    second_weight,
    halo0,
    halo1,
    halo2,
    halo3,
    agg0,
    agg1,
    agg2,
    agg3,
    prediction,
    grad_first,
    grad_second,
):
    halo = jnp.concatenate([part[...] for part in (halo0, halo1, halo2, halo3)], axis=0)
    halo_agg = jnp.concatenate([part[...] for part in (agg0, agg1, agg2, agg3)], axis=0)
    pre = dot(halo_agg, first_weight[...])
    sigm = jax.nn.sigmoid(pre)
    halo_slope = sigm * (1.0 + pre * (1.0 - sigm))
    halo_hidden = (halo.astype(jnp.float32) + pre * sigm).astype(jnp.bfloat16)
    second_agg = (inner[...] + dot(halo_bonds[...], halo_hidden)).astype(jnp.bfloat16)
    output = hidden[...].astype(jnp.float32) + dot(second_agg, second_weight[...])
    prediction[...] = output.astype(jnp.bfloat16)
    error = (output - targets[...].astype(jnp.float32)) * scale
    error_b = error.astype(jnp.bfloat16)
    grad_second[...] = dot_rows(second_agg, error_b)
    agg_cot = dot_last(error_b, second_weight[...]).astype(jnp.bfloat16)
    halo_cot = dot_rows(halo_bonds[...], agg_cot)
    halo_cot = (halo_cot * halo_slope).astype(jnp.bfloat16)
    own_cot = (error + dot_rows(bonds[...], agg_cot)) * slope[...]
    grad_first[...] = dot_rows(agg[...], own_cot.astype(jnp.bfloat16)) + dot_rows(
        halo_agg, halo_cot
    )


def summed(first, second):
    size = lax.axis_size("dom")
    even = lax.axis_index("dom") % 2 == 0
    total = jnp.where(even, first, second) + swapped(jnp.where(even, second, first), 1)
    mask = 2
    while mask < size:
        total = total + swapped(total, mask)
        mask *= 2
    other = swapped(total, 1)
    return jnp.where(even, total, other), jnp.where(even, other, total)


def local(
    features, targets, first_weight, second_weight, local_bonds, halo_bonds, tile_mask, send_rows
):
    atoms, wide = features.shape
    rounds, width = send_rows.shape
    low, high = jnp.bfloat16, jnp.float32
    sent = [((width, wide), low)] * rounds
    picker, *picked = call(
        pick_kernel, [((rounds * width, atoms), low)] + sent, features, send_rows
    )
    halo = [swapped(part, 2**turn) for turn, part in enumerate(picked)]
    bonds, inner = call(
        inner_kernel,
        [((atoms, atoms), low), ((atoms, wide), high)],
        local_bonds,
        tile_mask,
        features,
    )
    agg, *picked = call(
        first_kernel, [((atoms, wide), low)] + sent, inner, halo_bonds, picker, *halo
    )
    halo_agg = [swapped(part, 2**turn) for turn, part in enumerate(picked)]
    hidden, slope, inner = call(
        hidden_kernel,
        [((atoms, wide), low), ((atoms, wide), high), ((atoms, wide), high)],
        agg,
        first_weight,
        features,
        bonds,
    )
    scale = 1.0 / math.sqrt(atoms * lax.axis_size("dom"))
    prediction, grad_first, grad_second = call(
        functools.partial(back_kernel, scale),
        [((atoms, wide), low), ((wide, wide), high), ((wide, wide), high)],
        inner,
        hidden,
        slope,
        agg,
        bonds,
        halo_bonds,
        targets,
        first_weight,
        second_weight,
        *halo,
        *halo_agg,
    )
    grad_first, grad_second = summed(grad_first, grad_second)
    return prediction, grad_first, grad_second


def solution(mesh):
    rows = P("dom", None)
    in_specs = (rows, rows, P(), P(), rows, rows, rows, rows)
    out_specs = (rows, P(), P())
    return jax.shard_map(local, mesh=mesh, in_specs=in_specs, out_specs=out_specs, check_vma=False)
```

```python
import functools
import math

import jax
import jax.numpy as jnp
from jax import lax
from jax.experimental import pallas as pl
from jax.experimental.pallas import tpu as pltpu
from jax.sharding import PartitionSpec as P

TILE = 64
COST = pl.CostEstimate(flops=4 * 10**9, bytes_accessed=2**20, transcendentals=0)
PARAMS = pltpu.CompilerParams(vmem_limit_bytes=16 * 2**20)


def swapped(value, mask):
    pairs = [(source, source ^ mask) for source in range(lax.axis_size("dom"))]
    return lax.ppermute(value, "dom", pairs)


def dot(left, right):
    return jnp.dot(left, right, preferred_element_type=jnp.float32)


def dot_rows(left, right):
    return lax.dot_general(
        left, right, (((0,), (0,)), ((), ())), preferred_element_type=jnp.float32
    )


def dot_last(left, right):
    return lax.dot_general(
        left, right, (((1,), (1,)), ((), ())), preferred_element_type=jnp.float32
    )


def call(body, outs, *args, scratch=(), cost=None, remain=0):
    places = [pltpu.HBM] * remain + [pltpu.VMEM] * (len(args) - remain)
    args = [pltpu.with_memory_space_constraint(arg, place) for arg, place in zip(args, places)]
    return pl.pallas_call(
        body,
        out_shape=[pltpu.VMEM(shape, dtype) for shape, dtype in outs],
        in_specs=[pl.BlockSpec(memory_space=place) for place in places],
        out_specs=[pl.BlockSpec(memory_space=pltpu.VMEM)] * len(outs),
        scratch_shapes=list(scratch),
        cost_estimate=cost,
        compiler_params=PARAMS,
    )(*args)


def pick_kernel(features, send_rows, kept, picker, *rest):
    *picked, index, sems = rest
    rounds, width = send_rows.shape
    atoms = features.shape[0]
    indices = pltpu.make_async_copy(send_rows, index, sems.at[0])
    rows = pltpu.make_async_copy(features, kept, sems.at[1])
    indices.start()
    rows.start()
    column = lax.broadcasted_iota(jnp.int32, (width, atoms), 1)
    indices.wait()
    index = jnp.concatenate([index[...], jnp.zeros((8 - rounds, width), jnp.int32)], axis=0).T
    for turn in range(rounds):
        chosen = (index[:, turn : turn + 1] == column).astype(jnp.float32).astype(jnp.bfloat16)
        picker[turn * width : (turn + 1) * width, :] = chosen
    rows.wait()
    for turn, part in enumerate(picked):
        chosen = picker[turn * width : (turn + 1) * width, :]
        part[...] = dot(chosen, kept[...]).astype(jnp.bfloat16)


def inner_kernel(local_bonds, tile_mask, features, bonds, inner):
    tiles = tile_mask.shape[0]
    atoms = local_bonds.shape[0]
    spread = (
        lax.broadcasted_iota(jnp.int32, (tiles, atoms), 1) // TILE
        == lax.broadcasted_iota(jnp.int32, (tiles, atoms), 0)
    ).astype(jnp.float32).astype(jnp.bfloat16)
    wide = dot(tile_mask[...].astype(jnp.float32).astype(jnp.bfloat16), spread).astype(jnp.bfloat16)
    for tile in range(tiles):
        rows = slice(tile * TILE, (tile + 1) * TILE)
        bonds[rows, :] = local_bonds[rows, :] * wide[tile : tile + 1, :]
    inner[...] = dot(bonds[...], features[...])


def first_kernel(inner, halo_bonds, picker, *rest):
    rounds = len(rest) // 2 - 1
    halo, agg, picked, stacked = rest[:rounds], rest[rounds], rest[rounds + 1 : -1], rest[-1]
    width = halo[0].shape[0]
    for turn, part in enumerate(halo):
        stacked[turn * width : (turn + 1) * width, :] = part[...]
    agg[...] = (inner[...] + dot(halo_bonds[...], stacked[...])).astype(jnp.bfloat16)
    for turn, part in enumerate(picked):
        chosen = picker[turn * width : (turn + 1) * width, :]
        part[...] = dot(chosen, agg[...]).astype(jnp.bfloat16)


def hidden_kernel(agg, first_weight, features, bonds, hidden, slope, inner):
    pre = dot(agg[...], first_weight[...])
    sigm = jax.nn.sigmoid(pre)
    slope[...] = (sigm * (1.0 + pre * (1.0 - sigm))).T
    hidden[...] = (features[...].astype(jnp.float32) + pre * sigm).astype(jnp.bfloat16)
    inner[...] = dot(bonds[...], hidden[...])


def back_kernel(
    scale,
    inner,
    hidden,
    slope,
    agg,
    bonds,
    halo_bonds,
    targets,
    first_weight,
    second_weight,
    *rest,
):
    *halo, prediction, kept, given, halo_hidden, halo_agg = rest
    rounds = len(halo) // 2
    width = halo[0].shape[0]
    spans = [slice(turn * width, (turn + 1) * width) for turn in range(rounds)]
    for span, part in zip(spans, halo[rounds:]):
        halo_agg[span, :] = part[...]
    pre = dot(halo_agg[...], first_weight[...])
    sigm = jax.nn.sigmoid(pre)
    halo_slope = (sigm * (1.0 + pre * (1.0 - sigm))).T
    act = pre * sigm
    for span, part in zip(spans, halo[:rounds]):
        halo_hidden[span, :] = (part[...].astype(jnp.float32) + act[span]).astype(jnp.bfloat16)
    second_agg = (inner[...] + dot(halo_bonds[...], halo_hidden[...])).astype(jnp.bfloat16)
    output = hidden[...].astype(jnp.float32) + dot(second_agg, second_weight[...])
    prediction[...] = output.astype(jnp.bfloat16)
    error = (output - targets[...].astype(jnp.float32)) * scale
    error_b = error.astype(jnp.bfloat16)
    agg_cot = dot_last(second_weight[...], error_b).astype(jnp.bfloat16)
    halo_cot = (dot(agg_cot, halo_bonds[...]) * halo_slope).astype(jnp.bfloat16)
    own_cot = ((error.T + dot(agg_cot, bonds[...])) * slope[...]).astype(jnp.bfloat16)
    grad_first = (dot(halo_cot, halo_agg[...]) + dot(own_cot, agg[...])).T
    grad_second = dot_rows(second_agg, error_b)
    even = lax.rem(lax.axis_index("dom"), 2) == 0
    kept[...] = jnp.where(even, grad_first, grad_second)
    given[...] = jnp.where(even, grad_second, grad_first)


def split_kernel(total, other, grad_first, grad_second):
    even = lax.rem(lax.axis_index("dom"), 2) == 0
    grad_first[...] = jnp.where(even, total[...], other[...])
    grad_second[...] = jnp.where(even, other[...], total[...])


def summed(kept, given):
    total = kept + swapped(given, 1)
    mask = 2
    while mask < lax.axis_size("dom"):
        total = total + swapped(total, mask)
        mask *= 2
    whole = pl.BlockSpec(memory_space=pltpu.VMEM)
    return pl.pallas_call(
        split_kernel,
        out_shape=[jax.ShapeDtypeStruct(total.shape, total.dtype)] * 2,
        in_specs=[whole] * 2,
        out_specs=[whole] * 2,
        compiler_params=PARAMS,
    )(total, swapped(total, 1))


def local(
    features, targets, first_weight, second_weight, local_bonds, halo_bonds, tile_mask, send_rows
):
    atoms, wide = features.shape
    rounds, width = send_rows.shape
    low, high = jnp.bfloat16, jnp.float32
    sent = [((width, wide), low)] * rounds
    stacked = pltpu.VMEM((rounds * width, wide), low)
    features, picker, *picked = call(
        pick_kernel,
        [((atoms, wide), low), ((rounds * width, atoms), low)] + sent,
        features,
        send_rows,
        remain=2,
        scratch=[pltpu.VMEM((rounds, width), jnp.int32), pltpu.SemaphoreType.DMA((2,))],
        cost=COST,
    )
    halo = [swapped(part, 2**turn) for turn, part in enumerate(picked)]
    bonds, inner = call(
        inner_kernel,
        [((atoms, atoms), low), ((atoms, wide), high)],
        local_bonds,
        tile_mask,
        features,
    )
    agg, *picked = call(
        first_kernel,
        [((atoms, wide), low)] + sent,
        inner,
        halo_bonds,
        picker,
        *halo,
        scratch=[stacked],
    )
    halo_agg = [swapped(part, 2**turn) for turn, part in enumerate(picked)]
    hidden, slope, inner = call(
        hidden_kernel,
        [((atoms, wide), low), ((wide, atoms), high), ((atoms, wide), high)],
        agg,
        first_weight,
        features,
        bonds,
    )
    scale = 1.0 / math.sqrt(atoms * lax.axis_size("dom"))
    prediction, kept, given = call(
        functools.partial(back_kernel, scale),
        [((atoms, wide), low), ((wide, wide), high), ((wide, wide), high)],
        inner,
        hidden,
        slope,
        agg,
        bonds,
        halo_bonds,
        targets,
        first_weight,
        second_weight,
        *halo,
        *halo_agg,
        scratch=[stacked, stacked],
    )
    return (prediction, *summed(kept, given))


def solution(mesh):
    rows = P("dom", None)
    in_specs = (rows, rows, P(), P(), rows, rows, rows, rows)
    out_specs = (rows, P(), P())
    return jax.shard_map(local, mesh=mesh, in_specs=in_specs, out_specs=out_specs, check_vma=False)
```

```python
import functools
import math

import jax
import jax.numpy as jnp
from jax import lax
from jax.experimental import pallas as pl
from jax.experimental.pallas import tpu as pltpu
from jax.sharding import PartitionSpec as P

TILE = 64
COST = pl.CostEstimate(flops=4 * 10**9, bytes_accessed=2**20, transcendentals=0)
PARAMS = pltpu.CompilerParams(vmem_limit_bytes=16 * 2**20)


def swapped(value, mask):
    pairs = [(source, source ^ mask) for source in range(lax.axis_size("dom"))]
    return lax.ppermute(value, "dom", pairs)


def dot(left, right):
    return jnp.dot(left, right, preferred_element_type=jnp.float32)


def dot_rows(left, right):
    return lax.dot_general(
        left, right, (((0,), (0,)), ((), ())), preferred_element_type=jnp.float32
    )


def dot_last(left, right):
    return lax.dot_general(
        left, right, (((1,), (1,)), ((), ())), preferred_element_type=jnp.float32
    )


def call(body, outs, *args, scratch=(), cost=None, remain=0):
    places = [pltpu.HBM] * remain + [pltpu.VMEM] * (len(args) - remain)
    args = [pltpu.with_memory_space_constraint(arg, place) for arg, place in zip(args, places)]
    return pl.pallas_call(
        body,
        out_shape=[pltpu.VMEM(shape, dtype) for shape, dtype in outs],
        in_specs=[pl.BlockSpec(memory_space=place) for place in places],
        out_specs=[pl.BlockSpec(memory_space=pltpu.VMEM)] * len(outs),
        scratch_shapes=list(scratch),
        cost_estimate=cost,
        compiler_params=PARAMS,
    )(*args)


def pick_kernel(features, send_rows, kept, picker, *rest):
    *picked, index, sems = rest
    rounds, width = send_rows.shape
    atoms = features.shape[0]
    indices = pltpu.make_async_copy(send_rows, index, sems.at[0])
    rows = pltpu.make_async_copy(features, kept, sems.at[1])
    indices.start()
    rows.start()
    column = lax.broadcasted_iota(jnp.int32, (width, atoms), 1)
    indices.wait()
    index = jnp.concatenate([index[...], jnp.zeros((8 - rounds, width), jnp.int32)], axis=0).T
    for turn in range(rounds):
        chosen = (index[:, turn : turn + 1] == column).astype(jnp.float32).astype(jnp.bfloat16)
        picker[turn * width : (turn + 1) * width, :] = chosen
    rows.wait()
    for turn, part in enumerate(picked):
        chosen = picker[turn * width : (turn + 1) * width, :]
        part[...] = dot(chosen, kept[...]).astype(jnp.bfloat16)


def inner_kernel(
    local_bonds,
    tile_mask,
    features,
    halo_bonds,
    picker,
    send_rows,
    bonds,
    inner,
    inner_sent,
    halo_sent,
    index,
    sem,
):
    indices = pltpu.make_async_copy(send_rows, index, sem)
    indices.start()
    tiles = tile_mask.shape[0]
    atoms = local_bonds.shape[0]
    spread = (
        lax.broadcasted_iota(jnp.int32, (tiles, atoms), 1) // TILE
        == lax.broadcasted_iota(jnp.int32, (tiles, atoms), 0)
    ).astype(jnp.float32).astype(jnp.bfloat16)
    wide = dot(tile_mask[...].astype(jnp.float32).astype(jnp.bfloat16), spread).astype(jnp.bfloat16)
    for tile in range(tiles):
        rows = slice(tile * TILE, (tile + 1) * TILE)
        bonds[rows, :] = local_bonds[rows, :] * wide[tile : tile + 1, :]
    inner[...] = dot(bonds[...], features[...])
    halo_sent[...] = dot(picker[...], halo_bonds[...]).astype(jnp.bfloat16)
    indices.wait()
    rounds, width = index.shape
    for turn in range(rounds):
        for place in range(width):
            row = turn * width + place
            inner_sent[row : row + 1, :] = inner[pl.ds(index[turn, place], 1), :]


def sent_kernel(inner_sent, halo_sent, *rest):
    rounds = len(rest) // 2
    total = inner_sent[...]
    width = total.shape[0] // rounds
    for turn, part in enumerate(rest[:rounds]):
        total += dot(halo_sent[:, turn * width : (turn + 1) * width], part[...])
    for turn, part in enumerate(rest[rounds:]):
        part[...] = total[turn * width : (turn + 1) * width].astype(jnp.bfloat16)


def hidden_kernel(inner_first, halo_bonds, first_weight, features, bonds, *rest):
    *halo, agg, hidden, slope, inner, stacked = rest
    width = halo[0].shape[0]
    for turn, part in enumerate(halo):
        stacked[turn * width : (turn + 1) * width, :] = part[...]
    agg[...] = (inner_first[...] + dot(halo_bonds[...], stacked[...])).astype(jnp.bfloat16)
    pre = dot(agg[...], first_weight[...])
    sigm = jax.nn.sigmoid(pre)
    slope[...] = (sigm * (1.0 + pre * (1.0 - sigm))).T
    hidden[...] = (features[...].astype(jnp.float32) + pre * sigm).astype(jnp.bfloat16)
    inner[...] = dot(bonds[...], hidden[...])


def back_kernel(
    scale,
    inner,
    hidden,
    slope,
    agg,
    bonds,
    halo_bonds,
    targets,
    first_weight,
    second_weight,
    *rest,
):
    *halo, prediction, kept, given, halo_hidden, halo_agg = rest
    rounds = len(halo) // 2
    width = halo[0].shape[0]
    spans = [slice(turn * width, (turn + 1) * width) for turn in range(rounds)]
    for span, part in zip(spans, halo[rounds:]):
        halo_agg[span, :] = part[...]
    pre = dot(halo_agg[...], first_weight[...])
    sigm = jax.nn.sigmoid(pre)
    halo_slope = (sigm * (1.0 + pre * (1.0 - sigm))).T
    act = pre * sigm
    for span, part in zip(spans, halo[:rounds]):
        halo_hidden[span, :] = (part[...].astype(jnp.float32) + act[span]).astype(jnp.bfloat16)
    second_agg = (inner[...] + dot(halo_bonds[...], halo_hidden[...])).astype(jnp.bfloat16)
    output = hidden[...].astype(jnp.float32) + dot(second_agg, second_weight[...])
    prediction[...] = output.astype(jnp.bfloat16)
    error = (output - targets[...].astype(jnp.float32)) * scale
    error_b = error.astype(jnp.bfloat16)
    agg_cot = dot_last(second_weight[...], error_b).astype(jnp.bfloat16)
    halo_cot = (dot(agg_cot, halo_bonds[...]) * halo_slope).astype(jnp.bfloat16)
    own_cot = ((error.T + dot(agg_cot, bonds[...])) * slope[...]).astype(jnp.bfloat16)
    grad_first = (dot(halo_cot, halo_agg[...]) + dot(own_cot, agg[...])).T
    grad_second = dot_rows(second_agg, error_b)
    even = lax.rem(lax.axis_index("dom"), 2) == 0
    kept[...] = jnp.where(even, grad_first, grad_second)
    given[...] = jnp.where(even, grad_second, grad_first)


def split_kernel(total, other, grad_first, grad_second):
    even = lax.rem(lax.axis_index("dom"), 2) == 0
    grad_first[...] = jnp.where(even, total[...], other[...])
    grad_second[...] = jnp.where(even, other[...], total[...])


def summed(kept, given):
    total = kept + swapped(given, 1)
    size = lax.axis_size("dom")
    mask = 2
    while 2 * mask < size:
        near, far, both = (swapped(total, mask * way) for way in (1, 2, 3))
        total = (total + near) + (far + both)
        mask *= 4
    if mask < size:
        total = total + swapped(total, mask)
    whole = pl.BlockSpec(memory_space=pltpu.VMEM)
    return pl.pallas_call(
        split_kernel,
        out_shape=[jax.ShapeDtypeStruct(total.shape, total.dtype)] * 2,
        in_specs=[whole] * 2,
        out_specs=[whole] * 2,
        compiler_params=PARAMS,
    )(total, swapped(total, 1))


def local(
    features, targets, first_weight, second_weight, local_bonds, halo_bonds, tile_mask, send_rows
):
    atoms, wide = features.shape
    rounds, width = send_rows.shape
    low, high = jnp.bfloat16, jnp.float32
    sent = [((width, wide), low)] * rounds
    stacked = pltpu.VMEM((rounds * width, wide), low)
    features, picker, *picked = call(
        pick_kernel,
        [((atoms, wide), low), ((rounds * width, atoms), low)] + sent,
        features,
        send_rows,
        remain=2,
        scratch=[pltpu.VMEM((rounds, width), jnp.int32), pltpu.SemaphoreType.DMA((2,))],
        cost=COST,
    )
    halo = [swapped(part, 2**turn) for turn, part in enumerate(picked)]
    bonds, inner, inner_sent, halo_sent = call(
        inner_kernel,
        [
            ((atoms, atoms), low),
            ((atoms, wide), high),
            ((rounds * width, wide), high),
            ((rounds * width, rounds * width), low),
        ],
        local_bonds,
        tile_mask,
        features,
        halo_bonds,
        picker,
        send_rows,
        scratch=[pltpu.SMEM((rounds, width), jnp.int32), pltpu.SemaphoreType.DMA],
    )
    picked = call(sent_kernel, sent, inner_sent, halo_sent, *halo)
    halo_agg = [swapped(part, 2**turn) for turn, part in enumerate(picked)]
    agg, hidden, slope, inner = call(
        hidden_kernel,
        [
            ((atoms, wide), low),
            ((atoms, wide), low),
            ((wide, atoms), high),
            ((atoms, wide), high),
        ],
        inner,
        halo_bonds,
        first_weight,
        features,
        bonds,
        *halo,
        scratch=[stacked],
    )
    scale = 1.0 / math.sqrt(atoms * lax.axis_size("dom"))
    prediction, kept, given = call(
        functools.partial(back_kernel, scale),
        [((atoms, wide), low), ((wide, wide), high), ((wide, wide), high)],
        inner,
        hidden,
        slope,
        agg,
        bonds,
        halo_bonds,
        targets,
        first_weight,
        second_weight,
        *halo,
        *halo_agg,
        scratch=[stacked, stacked],
    )
    return (prediction, *summed(kept, given))


def solution(mesh):
    rows = P("dom", None)
    in_specs = (rows, rows, P(), P(), rows, rows, rows, rows)
    out_specs = (rows, P(), P())
    return jax.shard_map(local, mesh=mesh, in_specs=in_specs, out_specs=out_specs, check_vma=False)
```

```python
import functools
import math

import jax
import jax.numpy as jnp
from jax import lax
from jax.experimental import pallas as pl
from jax.experimental.pallas import tpu as pltpu
from jax.sharding import PartitionSpec as P

TILE = 64
COST = pl.CostEstimate(flops=4 * 10**9, bytes_accessed=2**20, transcendentals=0)
PARAMS = pltpu.CompilerParams(vmem_limit_bytes=16 * 2**20)


def swapped(value, mask):
    pairs = [(source, source ^ mask) for source in range(lax.axis_size("dom"))]
    return lax.ppermute(value, "dom", pairs)


def dot(left, right):
    return jnp.dot(left, right, preferred_element_type=jnp.float32)


def dot_rows(left, right):
    return lax.dot_general(
        left, right, (((0,), (0,)), ((), ())), preferred_element_type=jnp.float32
    )


def dot_last(left, right):
    return lax.dot_general(
        left, right, (((1,), (1,)), ((), ())), preferred_element_type=jnp.float32
    )


def call(body, outs, *args, scratch=(), cost=None, remain=0):
    places = [pltpu.HBM] * remain + [pltpu.VMEM] * (len(args) - remain)
    args = [pltpu.with_memory_space_constraint(arg, place) for arg, place in zip(args, places)]
    return pl.pallas_call(
        body,
        out_shape=[pltpu.VMEM(shape, dtype) for shape, dtype in outs],
        in_specs=[pl.BlockSpec(memory_space=place) for place in places],
        out_specs=[pl.BlockSpec(memory_space=pltpu.VMEM)] * len(outs),
        scratch_shapes=list(scratch),
        cost_estimate=cost,
        compiler_params=PARAMS,
    )(*args)


def pick_kernel(features, send_rows, kept, picker, *rest):
    *picked, index, sems = rest
    rounds, width = send_rows.shape
    atoms = features.shape[0]
    indices = pltpu.make_async_copy(send_rows, index, sems.at[0])
    rows = pltpu.make_async_copy(features, kept, sems.at[1])
    indices.start()
    rows.start()
    column = lax.broadcasted_iota(jnp.int32, (width, atoms), 1)
    indices.wait()
    index = jnp.concatenate([index[...], jnp.zeros((8 - rounds, width), jnp.int32)], axis=0).T
    for turn in range(rounds):
        chosen = (index[:, turn : turn + 1] == column).astype(jnp.float32).astype(jnp.bfloat16)
        picker[turn * width : (turn + 1) * width, :] = chosen
    rows.wait()
    for turn, part in enumerate(picked):
        chosen = picker[turn * width : (turn + 1) * width, :]
        part[...] = dot(chosen, kept[...]).astype(jnp.bfloat16)


def inner_kernel(
    local_bonds,
    tile_mask,
    features,
    halo_bonds,
    picker,
    send_rows,
    bonds,
    inner,
    inner_sent,
    halo_sent,
    index,
    sem,
):
    indices = pltpu.make_async_copy(send_rows, index, sem)
    indices.start()
    tiles = tile_mask.shape[0]
    atoms = local_bonds.shape[0]
    spread = (
        lax.broadcasted_iota(jnp.int32, (tiles, atoms), 1) // TILE
        == lax.broadcasted_iota(jnp.int32, (tiles, atoms), 0)
    ).astype(jnp.float32).astype(jnp.bfloat16)
    wide = dot(tile_mask[...].astype(jnp.float32).astype(jnp.bfloat16), spread).astype(jnp.bfloat16)
    for tile in range(tiles):
        rows = slice(tile * TILE, (tile + 1) * TILE)
        bonds[rows, :] = local_bonds[rows, :] * wide[tile : tile + 1, :]
    inner[...] = dot(bonds[...], features[...])
    halo_sent[...] = dot(picker[...], halo_bonds[...]).astype(jnp.bfloat16)
    indices.wait()
    rounds, width = index.shape
    for turn in range(rounds):
        for place in range(width):
            row = turn * width + place
            inner_sent[row : row + 1, :] = inner[pl.ds(index[turn, place], 1), :]


def sent_kernel(inner_sent, halo_sent, *rest):
    rounds = len(rest) // 2
    total = inner_sent[...]
    width = total.shape[0] // rounds
    for turn, part in enumerate(rest[:rounds]):
        total += dot(halo_sent[:, turn * width : (turn + 1) * width], part[...])
    for turn, part in enumerate(rest[rounds:]):
        part[...] = total[turn * width : (turn + 1) * width].astype(jnp.bfloat16)


def hidden_kernel(inner_first, halo_bonds, first_weight, features, bonds, *rest):
    *halo, agg, hidden, slope, inner, stacked = rest
    width = halo[0].shape[0]
    for turn, part in enumerate(halo):
        stacked[turn * width : (turn + 1) * width, :] = part[...]
    agg[...] = (inner_first[...] + dot(halo_bonds[...], stacked[...])).astype(jnp.bfloat16)
    pre = dot(agg[...], first_weight[...])
    sigm = jax.nn.sigmoid(pre)
    slope[...] = (sigm * (1.0 + pre * (1.0 - sigm))).T
    hidden[...] = (features[...].astype(jnp.float32) + pre * sigm).astype(jnp.bfloat16)
    inner[...] = dot(bonds[...], hidden[...])


def back_kernel(
    scale,
    inner,
    hidden,
    slope,
    agg,
    bonds,
    halo_bonds,
    targets,
    first_weight,
    second_weight,
    *rest,
):
    *halo, prediction, grads, halo_hidden, halo_agg = rest
    rounds = len(halo) // 2
    width = halo[0].shape[0]
    spans = [slice(turn * width, (turn + 1) * width) for turn in range(rounds)]
    for span, part in zip(spans, halo[rounds:]):
        halo_agg[span, :] = part[...]
    pre = dot(halo_agg[...], first_weight[...])
    sigm = jax.nn.sigmoid(pre)
    halo_slope = (sigm * (1.0 + pre * (1.0 - sigm))).T
    act = pre * sigm
    for span, part in zip(spans, halo[:rounds]):
        halo_hidden[span, :] = (part[...].astype(jnp.float32) + act[span]).astype(jnp.bfloat16)
    second_agg = (inner[...] + dot(halo_bonds[...], halo_hidden[...])).astype(jnp.bfloat16)
    output = hidden[...].astype(jnp.float32) + dot(second_agg, second_weight[...])
    prediction[...] = output.astype(jnp.bfloat16)
    error = (output - targets[...].astype(jnp.float32)) * scale
    error_b = error.astype(jnp.bfloat16)
    agg_cot = dot_last(second_weight[...], error_b).astype(jnp.bfloat16)
    halo_cot = (dot(agg_cot, halo_bonds[...]) * halo_slope).astype(jnp.bfloat16)
    own_cot = ((error.T + dot(agg_cot, bonds[...])) * slope[...]).astype(jnp.bfloat16)
    grad_first = (dot(halo_cot, halo_agg[...]) + dot(own_cot, agg[...])).T
    size = grad_first.shape[0]
    grads[:size, :] = grad_first
    grads[size:, :] = dot_rows(second_agg, error_b)


def summed(total):
    total = total + swapped(total, 1)
    size = lax.axis_size("dom")
    mask = 2
    while mask < size:
        low = total.astype(jnp.bfloat16)
        ways = (1, 2, 3) if 2 * mask < size else (1,)
        terms = [low, *(swapped(low, mask * way) for way in ways)]
        pairs = [term.astype(jnp.float32) for term in terms]
        while len(pairs) > 1:
            pairs = [left + right for left, right in zip(pairs[::2], pairs[1::2])]
        total = pairs[0]
        mask *= 4
    return total


def local(
    features, targets, first_weight, second_weight, local_bonds, halo_bonds, tile_mask, send_rows
):
    atoms, wide = features.shape
    rounds, width = send_rows.shape
    low, high = jnp.bfloat16, jnp.float32
    sent = [((width, wide), low)] * rounds
    stacked = pltpu.VMEM((rounds * width, wide), low)
    features, picker, *picked = call(
        pick_kernel,
        [((atoms, wide), low), ((rounds * width, atoms), low)] + sent,
        features,
        send_rows,
        remain=2,
        scratch=[pltpu.VMEM((rounds, width), jnp.int32), pltpu.SemaphoreType.DMA((2,))],
        cost=COST,
    )
    halo = [swapped(part, 2**turn) for turn, part in enumerate(picked)]
    bonds, inner, inner_sent, halo_sent = call(
        inner_kernel,
        [
            ((atoms, atoms), low),
            ((atoms, wide), high),
            ((rounds * width, wide), high),
            ((rounds * width, rounds * width), low),
        ],
        local_bonds,
        tile_mask,
        features,
        halo_bonds,
        picker,
        send_rows,
        scratch=[pltpu.SMEM((rounds, width), jnp.int32), pltpu.SemaphoreType.DMA],
    )
    picked = call(sent_kernel, sent, inner_sent, halo_sent, *halo)
    halo_agg = [swapped(part, 2**turn) for turn, part in enumerate(picked)]
    agg, hidden, slope, inner = call(
        hidden_kernel,
        [
            ((atoms, wide), low),
            ((atoms, wide), low),
            ((wide, atoms), high),
            ((atoms, wide), high),
        ],
        inner,
        halo_bonds,
        first_weight,
        features,
        bonds,
        *halo,
        scratch=[stacked],
    )
    scale = 1.0 / math.sqrt(atoms * lax.axis_size("dom"))
    prediction, grads = call(
        functools.partial(back_kernel, scale),
        [((atoms, wide), low), ((2 * wide, wide), high)],
        inner,
        hidden,
        slope,
        agg,
        bonds,
        halo_bonds,
        targets,
        first_weight,
        second_weight,
        *halo,
        *halo_agg,
        scratch=[stacked, stacked],
    )
    grads = summed(grads)
    return prediction, grads[:wide], grads[wide:]


def solution(mesh):
    rows = P("dom", None)
    in_specs = (rows, rows, P(), P(), rows, rows, rows, rows)
    out_specs = (rows, P(), P())
    return jax.shard_map(local, mesh=mesh, in_specs=in_specs, out_specs=out_specs, check_vma=False)
```

```python
import functools
import math

import jax
import jax.numpy as jnp
from jax import lax
from jax.experimental import pallas as pl
from jax.experimental.pallas import tpu as pltpu
from jax.sharding import PartitionSpec as P

TILE = 64
COST = pl.CostEstimate(flops=4 * 10**9, bytes_accessed=2**20, transcendentals=0)
PARAMS = pltpu.CompilerParams(vmem_limit_bytes=16 * 2**20)


def swapped(value, mask):
    pairs = [(source, source ^ mask) for source in range(lax.axis_size("dom"))]
    return lax.ppermute(value, "dom", pairs)


def dot(left, right):
    return jnp.dot(left, right, preferred_element_type=jnp.float32)


def dot_rows(left, right):
    return lax.dot_general(
        left, right, (((0,), (0,)), ((), ())), preferred_element_type=jnp.float32
    )


def dot_last(left, right):
    return lax.dot_general(
        left, right, (((1,), (1,)), ((), ())), preferred_element_type=jnp.float32
    )


def call(body, outs, *args, scratch=(), cost=None, remain=0):
    places = [pltpu.HBM] * remain + [pltpu.VMEM] * (len(args) - remain)
    args = [pltpu.with_memory_space_constraint(arg, place) for arg, place in zip(args, places)]
    return pl.pallas_call(
        body,
        out_shape=[pltpu.VMEM(shape, dtype) for shape, dtype in outs],
        in_specs=[pl.BlockSpec(memory_space=place) for place in places],
        out_specs=[pl.BlockSpec(memory_space=pltpu.VMEM)] * len(outs),
        scratch_shapes=list(scratch),
        cost_estimate=cost,
        compiler_params=PARAMS,
    )(*args)


def picker_kernel(features, send_rows, kept, picker, index, sems):
    rounds, width = send_rows.shape
    atoms = features.shape[0]
    indices = pltpu.make_async_copy(send_rows, index, sems.at[0])
    rows = pltpu.make_async_copy(features, kept, sems.at[1])
    indices.start()
    rows.start()
    column = lax.broadcasted_iota(jnp.int32, (width, atoms), 1)
    indices.wait()
    index = jnp.concatenate([index[...], jnp.zeros((8 - rounds, width), jnp.int32)], axis=0).T
    for turn in range(rounds):
        chosen = (index[:, turn : turn + 1] == column).astype(jnp.float32).astype(jnp.bfloat16)
        picker[turn * width : (turn + 1) * width, :] = chosen
    rows.wait()


def pick_kernel(picker, features, *picked):
    width = picked[0].shape[0]
    rows = dot(picker[...], features[...]).astype(jnp.bfloat16)
    for turn, part in enumerate(picked):
        part[...] = rows[turn * width : (turn + 1) * width]


def inner_kernel(
    local_bonds,
    tile_mask,
    features,
    halo_bonds,
    picker,
    send_rows,
    bonds,
    inner,
    inner_sent,
    halo_sent,
    index,
    sem,
):
    indices = pltpu.make_async_copy(send_rows, index, sem)
    indices.start()
    tiles = tile_mask.shape[0]
    atoms = local_bonds.shape[0]
    spread = (
        lax.broadcasted_iota(jnp.int32, (tiles, atoms), 1) // TILE
        == lax.broadcasted_iota(jnp.int32, (tiles, atoms), 0)
    ).astype(jnp.float32).astype(jnp.bfloat16)
    wide = dot(tile_mask[...].astype(jnp.float32).astype(jnp.bfloat16), spread).astype(jnp.bfloat16)
    for tile in range(tiles):
        rows = slice(tile * TILE, (tile + 1) * TILE)
        bonds[rows, :] = local_bonds[rows, :] * wide[tile : tile + 1, :]
    inner[...] = dot(bonds[...], features[...])
    halo_sent[...] = dot(picker[...], halo_bonds[...]).astype(jnp.bfloat16)
    indices.wait()
    rounds, width = index.shape
    for turn in range(rounds):
        for place in range(width):
            row = turn * width + place
            inner_sent[row : row + 1, :] = inner[pl.ds(index[turn, place], 1), :]


def sent_kernel(inner_sent, halo_sent, *rest):
    rounds = len(rest) // 2
    total = inner_sent[...]
    width = total.shape[0] // rounds
    for turn, part in enumerate(rest[:rounds]):
        total += dot(halo_sent[:, turn * width : (turn + 1) * width], part[...])
    for turn, part in enumerate(rest[rounds:]):
        part[...] = total[turn * width : (turn + 1) * width].astype(jnp.bfloat16)


def hidden_kernel(inner_first, halo_bonds, first_weight, features, bonds, *rest):
    *halo, agg, hidden, slope, inner, stacked = rest
    width = halo[0].shape[0]
    for turn, part in enumerate(halo):
        stacked[turn * width : (turn + 1) * width, :] = part[...]
    agg[...] = (inner_first[...] + dot(halo_bonds[...], stacked[...])).astype(jnp.bfloat16)
    pre = dot(agg[...], first_weight[...])
    sigm = jax.nn.sigmoid(pre)
    slope[...] = (sigm * (1.0 + pre * (1.0 - sigm))).T
    hidden[...] = (features[...].astype(jnp.float32) + pre * sigm).astype(jnp.bfloat16)
    inner[...] = dot(bonds[...], hidden[...])


def back_kernel(
    scale,
    inner,
    hidden,
    slope,
    agg,
    bonds,
    halo_bonds,
    targets,
    first_weight,
    second_weight,
    *rest,
):
    *halo, prediction, grads, halo_hidden, halo_agg = rest
    rounds = len(halo) // 2
    width = halo[0].shape[0]
    spans = [slice(turn * width, (turn + 1) * width) for turn in range(rounds)]
    for span, part in zip(spans, halo[rounds:]):
        halo_agg[span, :] = part[...]
    pre = dot(halo_agg[...], first_weight[...])
    sigm = jax.nn.sigmoid(pre)
    halo_slope = (sigm * (1.0 + pre * (1.0 - sigm))).T
    act = pre * sigm
    for span, part in zip(spans, halo[:rounds]):
        halo_hidden[span, :] = (part[...].astype(jnp.float32) + act[span]).astype(jnp.bfloat16)
    second_agg = (inner[...] + dot(halo_bonds[...], halo_hidden[...])).astype(jnp.bfloat16)
    output = hidden[...].astype(jnp.float32) + dot(second_agg, second_weight[...])
    prediction[...] = output.astype(jnp.bfloat16)
    error = (output - targets[...].astype(jnp.float32)) * scale
    error_b = error.astype(jnp.bfloat16)
    agg_cot = dot_last(second_weight[...], error_b).astype(jnp.bfloat16)
    halo_cot = (dot(agg_cot, halo_bonds[...]) * halo_slope).astype(jnp.bfloat16)
    own_cot = ((error.T + dot(agg_cot, bonds[...])) * slope[...]).astype(jnp.bfloat16)
    grad_first = (dot(halo_cot, halo_agg[...]) + dot(own_cot, agg[...])).T
    size = grad_first.shape[0]
    grads[:size, :] = grad_first
    grads[size:, :] = dot_rows(second_agg, error_b)


def summed(total):
    total = total + swapped(total, 1)
    size = lax.axis_size("dom")
    mask = 2
    while mask < size:
        low = total.astype(jnp.bfloat16)
        ways = (1, 2, 3) if 2 * mask < size else (1,)
        terms = [low, *(swapped(low, mask * way) for way in ways)]
        pairs = [term.astype(jnp.float32) for term in terms]
        while len(pairs) > 1:
            pairs = [left + right for left, right in zip(pairs[::2], pairs[1::2])]
        total = pairs[0]
        mask *= 4
    return total


def local(
    features, targets, first_weight, second_weight, local_bonds, halo_bonds, tile_mask, send_rows
):
    atoms, wide = features.shape
    rounds, width = send_rows.shape
    low, high = jnp.bfloat16, jnp.float32
    sent = [((width, wide), low)] * rounds
    stacked = pltpu.VMEM((rounds * width, wide), low)
    features, picker = call(
        picker_kernel,
        [((atoms, wide), low), ((rounds * width, atoms), low)],
        features,
        send_rows,
        remain=2,
        scratch=[pltpu.VMEM((rounds, width), jnp.int32), pltpu.SemaphoreType.DMA((2,))],
    )
    picked = call(pick_kernel, sent, picker, features, cost=COST)
    halo = [swapped(part, 2**turn) for turn, part in enumerate(picked)]
    bonds, inner, inner_sent, halo_sent = call(
        inner_kernel,
        [
            ((atoms, atoms), low),
            ((atoms, wide), high),
            ((rounds * width, wide), high),
            ((rounds * width, rounds * width), low),
        ],
        local_bonds,
        tile_mask,
        features,
        halo_bonds,
        picker,
        send_rows,
        scratch=[pltpu.SMEM((rounds, width), jnp.int32), pltpu.SemaphoreType.DMA],
    )
    picked = call(sent_kernel, sent, inner_sent, halo_sent, *halo)
    halo_agg = [swapped(part, 2**turn) for turn, part in enumerate(picked)]
    agg, hidden, slope, inner = call(
        hidden_kernel,
        [
            ((atoms, wide), low),
            ((atoms, wide), low),
            ((wide, atoms), high),
            ((atoms, wide), high),
        ],
        inner,
        halo_bonds,
        first_weight,
        features,
        bonds,
        *halo,
        scratch=[stacked],
    )
    scale = 1.0 / math.sqrt(atoms * lax.axis_size("dom"))
    prediction, grads = call(
        functools.partial(back_kernel, scale),
        [((atoms, wide), low), ((2 * wide, wide), high)],
        inner,
        hidden,
        slope,
        agg,
        bonds,
        halo_bonds,
        targets,
        first_weight,
        second_weight,
        *halo,
        *halo_agg,
        scratch=[stacked, stacked],
    )
    grads = summed(grads)
    return prediction, grads[:wide], grads[wide:]


def solution(mesh):
    rows = P("dom", None)
    in_specs = (rows, rows, P(), P(), rows, rows, rows, rows)
    out_specs = (rows, P(), P())
    return jax.shard_map(local, mesh=mesh, in_specs=in_specs, out_specs=out_specs, check_vma=False)
```

```python
import functools
import math

import jax
import jax.numpy as jnp
from jax import lax
from jax.experimental import pallas as pl
from jax.experimental.pallas import tpu as pltpu
from jax.sharding import PartitionSpec as P

TILE = 64
COST = pl.CostEstimate(flops=4 * 10**9, bytes_accessed=2**20, transcendentals=0)
PARAMS = pltpu.CompilerParams(vmem_limit_bytes=16 * 2**20)


def swapped(value, mask):
    pairs = [(source, source ^ mask) for source in range(lax.axis_size("dom"))]
    return lax.ppermute(value, "dom", pairs)


def dot(left, right):
    return jnp.dot(left, right, preferred_element_type=jnp.float32)


def dot_rows(left, right):
    return lax.dot_general(
        left, right, (((0,), (0,)), ((), ())), preferred_element_type=jnp.float32
    )


def dot_last(left, right):
    return lax.dot_general(
        left, right, (((1,), (1,)), ((), ())), preferred_element_type=jnp.float32
    )


def call(body, outs, *args, scratch=(), cost=None, remain=0):
    places = [pltpu.HBM] * remain + [pltpu.VMEM] * (len(args) - remain)
    args = [pltpu.with_memory_space_constraint(arg, place) for arg, place in zip(args, places)]
    return pl.pallas_call(
        body,
        out_shape=[pltpu.VMEM(shape, dtype) for shape, dtype in outs],
        in_specs=[pl.BlockSpec(memory_space=place) for place in places],
        out_specs=[pl.BlockSpec(memory_space=pltpu.VMEM)] * len(outs),
        scratch_shapes=list(scratch),
        cost_estimate=cost,
        compiler_params=PARAMS,
    )(*args)


def picker_kernel(features, send_rows, kept, picker, index, sems):
    rounds, width = send_rows.shape
    atoms = features.shape[0]
    indices = pltpu.make_async_copy(send_rows, index, sems.at[0])
    rows = pltpu.make_async_copy(features, kept, sems.at[1])
    indices.start()
    rows.start()
    column = lax.broadcasted_iota(jnp.int32, (width, atoms), 1)
    indices.wait()
    index = jnp.concatenate([index[...], jnp.zeros((8 - rounds, width), jnp.int32)], axis=0).T
    for turn in range(rounds):
        chosen = (index[:, turn : turn + 1] == column).astype(jnp.float32).astype(jnp.bfloat16)
        picker[turn * width : (turn + 1) * width, :] = chosen
    rows.wait()


def pick_kernel(picker, features, *picked):
    width = picked[0].shape[0]
    rows = dot(picker[...], features[...]).astype(jnp.bfloat16)
    for turn, part in enumerate(picked):
        part[...] = rows[turn * width : (turn + 1) * width]


def inner_kernel(
    local_bonds,
    tile_mask,
    features,
    halo_bonds,
    picker,
    send_rows,
    bonds,
    inner,
    inner_sent,
    halo_sent,
    index,
    sem,
):
    indices = pltpu.make_async_copy(send_rows, index, sem)
    indices.start()
    tiles = tile_mask.shape[0]
    atoms = local_bonds.shape[0]
    spread = (
        lax.broadcasted_iota(jnp.int32, (tiles, atoms), 1) // TILE
        == lax.broadcasted_iota(jnp.int32, (tiles, atoms), 0)
    ).astype(jnp.float32).astype(jnp.bfloat16)
    wide = dot(tile_mask[...].astype(jnp.float32).astype(jnp.bfloat16), spread).astype(jnp.bfloat16)
    for tile in range(tiles):
        rows = slice(tile * TILE, (tile + 1) * TILE)
        bonds[rows, :] = local_bonds[rows, :] * wide[tile : tile + 1, :]
    inner[...] = dot(bonds[...], features[...])
    halo_sent[...] = dot(picker[...], halo_bonds[...]).astype(jnp.bfloat16)
    indices.wait()
    rounds, width = index.shape
    for turn in range(rounds):
        for place in range(width):
            row = turn * width + place
            inner_sent[row : row + 1, :] = inner[pl.ds(index[turn, place], 1), :]


def sent_kernel(inner_sent, halo_sent, *rest):
    rounds = len(rest) // 2
    total = inner_sent[...]
    width = total.shape[0] // rounds
    for turn, part in enumerate(rest[:rounds]):
        total += dot(halo_sent[:, turn * width : (turn + 1) * width], part[...])
    for turn, part in enumerate(rest[rounds:]):
        part[...] = total[turn * width : (turn + 1) * width].astype(jnp.bfloat16)


def hidden_kernel(inner_first, halo_bonds, first_weight, features, bonds, *rest):
    *halo, agg, hidden, slope, inner, stacked = rest
    width = halo[0].shape[0]
    for turn, part in enumerate(halo):
        stacked[turn * width : (turn + 1) * width, :] = part[...]
    agg[...] = (inner_first[...] + dot(halo_bonds[...], stacked[...])).astype(jnp.bfloat16)
    pre = dot(agg[...], first_weight[...])
    sigm = jax.nn.sigmoid(pre)
    slope[...] = (sigm * (1.0 + pre * (1.0 - sigm))).T
    hidden[...] = (features[...].astype(jnp.float32) + pre * sigm).astype(jnp.bfloat16)
    inner[...] = dot(bonds[...], hidden[...])


def back_kernel(
    scale,
    inner,
    hidden,
    slope,
    agg,
    bonds,
    halo_bonds,
    targets,
    first_weight,
    second_weight,
    *rest,
):
    *halo, prediction, grads, halo_hidden, halo_agg = rest
    rounds = len(halo) // 2
    width = halo[0].shape[0]
    spans = [slice(turn * width, (turn + 1) * width) for turn in range(rounds)]
    for span, part in zip(spans, halo[rounds:]):
        halo_agg[span, :] = part[...]
    pre = dot(halo_agg[...], first_weight[...])
    sigm = jax.nn.sigmoid(pre)
    halo_slope = (sigm * (1.0 + pre * (1.0 - sigm))).T
    act = pre * sigm
    for span, part in zip(spans, halo[:rounds]):
        halo_hidden[span, :] = (part[...].astype(jnp.float32) + act[span]).astype(jnp.bfloat16)
    second_agg = (inner[...] + dot(halo_bonds[...], halo_hidden[...])).astype(jnp.bfloat16)
    output = hidden[...].astype(jnp.float32) + dot(second_agg, second_weight[...])
    prediction[...] = output.astype(jnp.bfloat16)
    error = (output - targets[...].astype(jnp.float32)) * scale
    error_b = error.astype(jnp.bfloat16)
    agg_cot = dot_last(second_weight[...], error_b).astype(jnp.bfloat16)
    halo_cot = (dot(agg_cot, halo_bonds[...]) * halo_slope).astype(jnp.bfloat16)
    own_cot = ((error.T + dot(agg_cot, bonds[...])) * slope[...]).astype(jnp.bfloat16)
    grad_first = (dot(halo_cot, halo_agg[...]) + dot(own_cot, agg[...])).T
    size = grad_first.shape[0]
    grads[:size, :] = grad_first
    grads[size:, :] = dot_rows(second_agg, error_b)


def mixed(value, even_mask, odd_mask):
    masks = (even_mask, odd_mask)
    pairs = [(source, source ^ masks[source % 2]) for source in range(lax.axis_size("dom"))]
    return lax.ppermute(value, "dom", pairs)


def four_kernel(own, first, second, third, total):
    even = lax.rem(lax.axis_index("dom"), 2) == 0
    own, first, second, third = (
        part[...].astype(jnp.float32) for part in (own, first, second, third)
    )
    total[...] = jnp.where(even, (own + first) + (second + third), (own + second) + (first + third))


def half_kernel(own, near, far, half):
    even = lax.rem(lax.axis_index("dom"), 2) == 0
    mine = jnp.where(even, own[...].astype(jnp.float32), far[...].astype(jnp.float32))
    half[...] = mine + near[...].astype(jnp.float32)


def summed(total):
    size = lax.axis_size("dom")
    wide = [(total.shape, jnp.float32)]
    total = total + swapped(total, 1)
    mask = 2
    while mask < size:
        low = total.astype(jnp.bfloat16)
        if 2 * mask >= size:
            total = low.astype(jnp.float32) + swapped(low, mask).astype(jnp.float32)
        elif mask == 2:
            terms = [
                mixed(low, mask, 2 * mask),
                mixed(low, 2 * mask, mask),
                mixed(low, 3 * mask, 3 * mask),
            ]
            (total,) = call(four_kernel, wide, low, *terms)
        else:
            near, far = mixed(low, mask, 2 * mask), mixed(low, mask, 3 * mask)
            (half,) = call(half_kernel, wide, low, near, far)
            total = half + swapped(half, 1)
        mask *= 4
    return total


def local(
    features, targets, first_weight, second_weight, local_bonds, halo_bonds, tile_mask, send_rows
):
    atoms, wide = features.shape
    rounds, width = send_rows.shape
    low, high = jnp.bfloat16, jnp.float32
    sent = [((width, wide), low)] * rounds
    stacked = pltpu.VMEM((rounds * width, wide), low)
    features, picker = call(
        picker_kernel,
        [((atoms, wide), low), ((rounds * width, atoms), low)],
        features,
        send_rows,
        remain=2,
        scratch=[pltpu.VMEM((rounds, width), jnp.int32), pltpu.SemaphoreType.DMA((2,))],
    )
    picked = call(pick_kernel, sent, picker, features, cost=COST)
    halo = [swapped(part, 2**turn) for turn, part in enumerate(picked)]
    bonds, inner, inner_sent, halo_sent = call(
        inner_kernel,
        [
            ((atoms, atoms), low),
            ((atoms, wide), high),
            ((rounds * width, wide), high),
            ((rounds * width, rounds * width), low),
        ],
        local_bonds,
        tile_mask,
        features,
        halo_bonds,
        picker,
        send_rows,
        scratch=[pltpu.SMEM((rounds, width), jnp.int32), pltpu.SemaphoreType.DMA],
    )
    picked = call(sent_kernel, sent, inner_sent, halo_sent, *halo)
    halo_agg = [swapped(part, 2**turn) for turn, part in enumerate(picked)]
    agg, hidden, slope, inner = call(
        hidden_kernel,
        [
            ((atoms, wide), low),
            ((atoms, wide), low),
            ((wide, atoms), high),
            ((atoms, wide), high),
        ],
        inner,
        halo_bonds,
        first_weight,
        features,
        bonds,
        *halo,
        scratch=[stacked],
    )
    scale = 1.0 / math.sqrt(atoms * lax.axis_size("dom"))
    prediction, grads = call(
        functools.partial(back_kernel, scale),
        [((atoms, wide), low), ((2 * wide, wide), high)],
        inner,
        hidden,
        slope,
        agg,
        bonds,
        halo_bonds,
        targets,
        first_weight,
        second_weight,
        *halo,
        *halo_agg,
        scratch=[stacked, stacked],
    )
    grads = summed(grads)
    return prediction, grads[:wide], grads[wide:]


def solution(mesh):
    rows = P("dom", None)
    in_specs = (rows, rows, P(), P(), rows, rows, rows, rows)
    out_specs = (rows, P(), P())
    return jax.shard_map(local, mesh=mesh, in_specs=in_specs, out_specs=out_specs, check_vma=False)
```

```python
import functools
import math

import jax
import jax.numpy as jnp
from jax import lax
from jax.experimental import pallas as pl
from jax.experimental.pallas import tpu as pltpu
from jax.sharding import PartitionSpec as P

TILE = 64
COST = pl.CostEstimate(flops=4 * 10**9, bytes_accessed=2**20, transcendentals=0)
PARAMS = pltpu.CompilerParams(vmem_limit_bytes=16 * 2**20)


def swapped(value, mask):
    pairs = [(source, source ^ mask) for source in range(lax.axis_size("dom"))]
    return lax.ppermute(value, "dom", pairs)


def dot(left, right):
    return jnp.dot(left, right, preferred_element_type=jnp.float32)


def dot_rows(left, right):
    return lax.dot_general(
        left, right, (((0,), (0,)), ((), ())), preferred_element_type=jnp.float32
    )


def dot_last(left, right):
    return lax.dot_general(
        left, right, (((1,), (1,)), ((), ())), preferred_element_type=jnp.float32
    )


def call(body, outs, *args, scratch=(), cost=None, remain=0):
    places = [pltpu.HBM] * remain + [pltpu.VMEM] * (len(args) - remain)
    args = [pltpu.with_memory_space_constraint(arg, place) for arg, place in zip(args, places)]
    return pl.pallas_call(
        body,
        out_shape=[pltpu.VMEM(shape, dtype) for shape, dtype in outs],
        in_specs=[pl.BlockSpec(memory_space=place) for place in places],
        out_specs=[pl.BlockSpec(memory_space=pltpu.VMEM)] * len(outs),
        scratch_shapes=list(scratch),
        cost_estimate=cost,
        compiler_params=PARAMS,
    )(*args)


def picker_kernel(features, send_rows, kept, picker, index, sems):
    rounds, width = send_rows.shape
    atoms = features.shape[0]
    indices = pltpu.make_async_copy(send_rows, index, sems.at[0])
    rows = pltpu.make_async_copy(features, kept, sems.at[1])
    indices.start()
    rows.start()
    column = lax.broadcasted_iota(jnp.int32, (width, atoms), 1)
    indices.wait()
    index = jnp.concatenate([index[...], jnp.zeros((8 - rounds, width), jnp.int32)], axis=0).T
    for turn in range(rounds):
        chosen = (index[:, turn : turn + 1] == column).astype(jnp.float32).astype(jnp.bfloat16)
        picker[turn * width : (turn + 1) * width, :] = chosen
    rows.wait()


def pick_kernel(picker, features, *picked):
    width = picked[0].shape[0]
    rows = dot(picker[...], features[...]).astype(jnp.bfloat16)
    for turn, part in enumerate(picked):
        part[...] = rows[turn * width : (turn + 1) * width]


def inner_kernel(
    local_bonds,
    tile_mask,
    features,
    halo_bonds,
    picker,
    send_rows,
    bonds,
    inner,
    inner_sent,
    halo_sent,
    index,
    sem,
):
    indices = pltpu.make_async_copy(send_rows, index, sem)
    indices.start()
    tiles = tile_mask.shape[0]
    atoms = local_bonds.shape[0]
    spread = (
        lax.broadcasted_iota(jnp.int32, (tiles, atoms), 1) // TILE
        == lax.broadcasted_iota(jnp.int32, (tiles, atoms), 0)
    ).astype(jnp.float32).astype(jnp.bfloat16)
    wide = dot(tile_mask[...].astype(jnp.float32).astype(jnp.bfloat16), spread).astype(jnp.bfloat16)
    for tile in range(tiles):
        rows = slice(tile * TILE, (tile + 1) * TILE)
        bonds[rows, :] = local_bonds[rows, :] * wide[tile : tile + 1, :]
    inner[...] = dot(bonds[...], features[...])
    halo_sent[...] = dot(picker[...], halo_bonds[...]).astype(jnp.bfloat16)
    indices.wait()
    rounds, width = index.shape
    for turn in range(rounds):
        for place in range(width):
            row = turn * width + place
            inner_sent[row : row + 1, :] = inner[pl.ds(index[turn, place], 1), :]


def sent_kernel(inner_sent, halo_sent, *rest):
    rounds = len(rest) // 2
    total = inner_sent[...]
    width = total.shape[0] // rounds
    for turn, part in enumerate(rest[:rounds]):
        total += dot(halo_sent[:, turn * width : (turn + 1) * width], part[...])
    for turn, part in enumerate(rest[rounds:]):
        part[...] = total[turn * width : (turn + 1) * width].astype(jnp.bfloat16)


def hidden_kernel(inner_first, halo_bonds, first_weight, features, bonds, *rest):
    *halo, agg, hidden, slope, inner, stacked = rest
    width = halo[0].shape[0]
    for turn, part in enumerate(halo):
        stacked[turn * width : (turn + 1) * width, :] = part[...]
    agg[...] = (inner_first[...] + dot(halo_bonds[...], stacked[...])).astype(jnp.bfloat16)
    pre = dot(agg[...], first_weight[...])
    sigm = jax.nn.sigmoid(pre)
    slope[...] = (sigm * (1.0 + pre * (1.0 - sigm))).T
    hidden[...] = (features[...].astype(jnp.float32) + pre * sigm).astype(jnp.bfloat16)
    inner[...] = dot(bonds[...], hidden[...])


def back_kernel(
    scale,
    inner,
    hidden,
    slope,
    agg,
    bonds,
    halo_bonds,
    targets,
    first_weight,
    second_weight,
    *rest,
):
    *halo, prediction, grads, halo_hidden, halo_agg = rest
    rounds = len(halo) // 2
    width = halo[0].shape[0]
    spans = [slice(turn * width, (turn + 1) * width) for turn in range(rounds)]
    for span, part in zip(spans, halo[rounds:]):
        halo_agg[span, :] = part[...]
    pre = dot(halo_agg[...], first_weight[...])
    sigm = jax.nn.sigmoid(pre)
    halo_slope = (sigm * (1.0 + pre * (1.0 - sigm))).T
    act = pre * sigm
    for span, part in zip(spans, halo[:rounds]):
        halo_hidden[span, :] = (part[...].astype(jnp.float32) + act[span]).astype(jnp.bfloat16)
    second_agg = (inner[...] + dot(halo_bonds[...], halo_hidden[...])).astype(jnp.bfloat16)
    output = hidden[...].astype(jnp.float32) + dot(second_agg, second_weight[...])
    prediction[...] = output.astype(jnp.bfloat16)
    error = (output - targets[...].astype(jnp.float32)) * scale
    error_b = error.astype(jnp.bfloat16)
    agg_cot = dot_last(second_weight[...], error_b).astype(jnp.bfloat16)
    halo_cot = (dot(agg_cot, halo_bonds[...]) * halo_slope).astype(jnp.bfloat16)
    own_cot = ((error.T + dot(agg_cot, bonds[...])) * slope[...]).astype(jnp.bfloat16)
    grad_first = (dot(halo_cot, halo_agg[...]) + dot(own_cot, agg[...])).T
    size = grad_first.shape[0]
    grads[:size, :] = grad_first
    grads[size:, :] = dot_rows(second_agg, error_b)


def mixed(value, even_mask, odd_mask):
    masks = (even_mask, odd_mask)
    pairs = [(source, source ^ masks[source % 2]) for source in range(lax.axis_size("dom"))]
    return lax.ppermute(value, "dom", pairs)


def four_kernel(own, first, second, third, total):
    even = lax.rem(lax.axis_index("dom"), 2) == 0
    own, first, second, third = (
        part[...].astype(jnp.float32) for part in (own, first, second, third)
    )
    summed_up = jnp.where(even, (own + first) + (second + third), (own + second) + (first + third))
    total[...] = summed_up.astype(total.dtype)


def half_kernel(own, near, far, half):
    even = lax.rem(lax.axis_index("dom"), 2) == 0
    mine = jnp.where(even, own[...].astype(jnp.float32), far[...].astype(jnp.float32))
    half[...] = mine + near[...].astype(jnp.float32)


def summed(total):
    size = lax.axis_size("dom")
    wide = [(total.shape, jnp.float32)]
    total = total + swapped(total, 1)
    mask = 2
    while mask < size:
        low = total.astype(jnp.bfloat16)
        if 2 * mask >= size:
            total = low.astype(jnp.float32) + swapped(low, mask).astype(jnp.float32)
        elif mask == 2:
            terms = [
                mixed(low, mask, 2 * mask),
                mixed(low, 2 * mask, mask),
                mixed(low, 3 * mask, 3 * mask),
            ]
            kind = low.dtype if 4 * mask < size else jnp.float32
            (total,) = call(four_kernel, [(low.shape, kind)], low, *terms)
        else:
            near, far = mixed(low, mask, 2 * mask), mixed(low, mask, 3 * mask)
            (half,) = call(half_kernel, wide, low, near, far)
            total = half + swapped(half, 1)
        mask *= 4
    return total


def local(
    features, targets, first_weight, second_weight, local_bonds, halo_bonds, tile_mask, send_rows
):
    atoms, wide = features.shape
    rounds, width = send_rows.shape
    low, high = jnp.bfloat16, jnp.float32
    sent = [((width, wide), low)] * rounds
    stacked = pltpu.VMEM((rounds * width, wide), low)
    features, picker = call(
        picker_kernel,
        [((atoms, wide), low), ((rounds * width, atoms), low)],
        features,
        send_rows,
        remain=2,
        scratch=[pltpu.VMEM((rounds, width), jnp.int32), pltpu.SemaphoreType.DMA((2,))],
    )
    picked = call(pick_kernel, sent, picker, features, cost=COST)
    halo = [swapped(part, 2**turn) for turn, part in enumerate(picked)]
    bonds, inner, inner_sent, halo_sent = call(
        inner_kernel,
        [
            ((atoms, atoms), low),
            ((atoms, wide), high),
            ((rounds * width, wide), high),
            ((rounds * width, rounds * width), low),
        ],
        local_bonds,
        tile_mask,
        features,
        halo_bonds,
        picker,
        send_rows,
        scratch=[pltpu.SMEM((rounds, width), jnp.int32), pltpu.SemaphoreType.DMA],
    )
    picked = call(sent_kernel, sent, inner_sent, halo_sent, *halo)
    halo_agg = [swapped(part, 2**turn) for turn, part in enumerate(picked)]
    agg, hidden, slope, inner = call(
        hidden_kernel,
        [
            ((atoms, wide), low),
            ((atoms, wide), low),
            ((wide, atoms), high),
            ((atoms, wide), high),
        ],
        inner,
        halo_bonds,
        first_weight,
        features,
        bonds,
        *halo,
        scratch=[stacked],
    )
    scale = 1.0 / math.sqrt(atoms * lax.axis_size("dom"))
    prediction, grads = call(
        functools.partial(back_kernel, scale),
        [((atoms, wide), low), ((2 * wide, wide), high)],
        inner,
        hidden,
        slope,
        agg,
        bonds,
        halo_bonds,
        targets,
        first_weight,
        second_weight,
        *halo,
        *halo_agg,
        scratch=[stacked, stacked],
    )
    grads = summed(grads)
    return prediction, grads[:wide], grads[wide:]


def solution(mesh):
    rows = P("dom", None)
    in_specs = (rows, rows, P(), P(), rows, rows, rows, rows)
    out_specs = (rows, P(), P())
    return jax.shard_map(local, mesh=mesh, in_specs=in_specs, out_specs=out_specs, check_vma=False)
```

```python
import functools
import math

import jax
import jax.numpy as jnp
from jax import lax
from jax.experimental import pallas as pl
from jax.experimental.pallas import tpu as pltpu
from jax.sharding import PartitionSpec as P

TILE = 64
COST = pl.CostEstimate(flops=4 * 10**9, bytes_accessed=2**20, transcendentals=0)
PARAMS = pltpu.CompilerParams(vmem_limit_bytes=16 * 2**20)


def swapped(value, mask):
    pairs = [(source, source ^ mask) for source in range(lax.axis_size("dom"))]
    return lax.ppermute(value, "dom", pairs)


def dot(left, right):
    return jnp.dot(left, right, preferred_element_type=jnp.float32)


def dot_rows(left, right):
    return lax.dot_general(
        left, right, (((0,), (0,)), ((), ())), preferred_element_type=jnp.float32
    )


def dot_last(left, right):
    return lax.dot_general(
        left, right, (((1,), (1,)), ((), ())), preferred_element_type=jnp.float32
    )


def call(body, outs, *args, scratch=(), cost=None, remain=0):
    places = [pltpu.HBM] * remain + [pltpu.VMEM] * (len(args) - remain)
    args = [pltpu.with_memory_space_constraint(arg, place) for arg, place in zip(args, places)]
    return pl.pallas_call(
        body,
        out_shape=[pltpu.VMEM(shape, dtype) for shape, dtype in outs],
        in_specs=[pl.BlockSpec(memory_space=place) for place in places],
        out_specs=[pl.BlockSpec(memory_space=pltpu.VMEM)] * len(outs),
        scratch_shapes=list(scratch),
        cost_estimate=cost,
        compiler_params=PARAMS,
    )(*args)


def picker_kernel(features, send_rows, kept, picker, index, sems):
    rounds, width = send_rows.shape
    atoms = features.shape[0]
    indices = pltpu.make_async_copy(send_rows, index, sems.at[0])
    rows = pltpu.make_async_copy(features, kept, sems.at[1])
    indices.start()
    rows.start()
    column = lax.broadcasted_iota(jnp.int32, (width, atoms), 1)
    indices.wait()
    index = jnp.concatenate([index[...], jnp.zeros((8 - rounds, width), jnp.int32)], axis=0).T
    for turn in range(rounds):
        chosen = (index[:, turn : turn + 1] == column).astype(jnp.float32).astype(jnp.bfloat16)
        picker[turn * width : (turn + 1) * width, :] = chosen
    rows.wait()


def pick_kernel(picker, features, *picked):
    width = picked[0].shape[0]
    rows = dot(picker[...], features[...]).astype(jnp.bfloat16)
    for turn, part in enumerate(picked):
        part[...] = rows[turn * width : (turn + 1) * width]


def inner_kernel(
    local_bonds,
    tile_mask,
    features,
    halo_bonds,
    picker,
    send_rows,
    bonds,
    inner,
    inner_sent,
    halo_sent,
    index,
    sem,
):
    indices = pltpu.make_async_copy(send_rows, index, sem)
    indices.start()
    tiles = tile_mask.shape[0]
    atoms = local_bonds.shape[0]
    spread = (
        lax.broadcasted_iota(jnp.int32, (tiles, atoms), 1) // TILE
        == lax.broadcasted_iota(jnp.int32, (tiles, atoms), 0)
    ).astype(jnp.float32).astype(jnp.bfloat16)
    wide = dot(tile_mask[...].astype(jnp.float32).astype(jnp.bfloat16), spread).astype(jnp.bfloat16)
    for tile in range(tiles):
        rows = slice(tile * TILE, (tile + 1) * TILE)
        bonds[rows, :] = local_bonds[rows, :] * wide[tile : tile + 1, :]
    inner[...] = dot(bonds[...], features[...])
    halo_sent[...] = dot(picker[...], halo_bonds[...]).astype(jnp.bfloat16)
    indices.wait()
    rounds, width = index.shape
    for turn in range(rounds):
        for place in range(width):
            row = turn * width + place
            inner_sent[row : row + 1, :] = inner[pl.ds(index[turn, place], 1), :]


def sent_kernel(inner_sent, halo_sent, *rest):
    rounds = len(rest) // 2
    total = inner_sent[...]
    width = total.shape[0] // rounds
    for turn, part in enumerate(rest[:rounds]):
        total += dot(halo_sent[:, turn * width : (turn + 1) * width], part[...])
    for turn, part in enumerate(rest[rounds:]):
        part[...] = total[turn * width : (turn + 1) * width].astype(jnp.bfloat16)


def hidden_kernel(inner_first, halo_bonds, first_weight, features, bonds, *rest):
    *halo, agg, hidden, slope, inner, stacked = rest
    width = halo[0].shape[0]
    for turn, part in enumerate(halo):
        stacked[turn * width : (turn + 1) * width, :] = part[...]
    agg[...] = (inner_first[...] + dot(halo_bonds[...], stacked[...])).astype(jnp.bfloat16)
    pre = dot(agg[...], first_weight[...])
    sigm = jax.nn.sigmoid(pre)
    slope[...] = (sigm * (1.0 + pre * (1.0 - sigm))).T
    hidden[...] = (features[...].astype(jnp.float32) + pre * sigm).astype(jnp.bfloat16)
    inner[...] = dot(bonds[...], hidden[...])


def back_kernel(
    scale,
    inner,
    hidden,
    slope,
    agg,
    bonds,
    halo_bonds,
    targets,
    first_weight,
    second_weight,
    *rest,
):
    *halo, prediction, grads, halo_hidden, halo_agg = rest
    rounds = len(halo) // 2
    width = halo[0].shape[0]
    spans = [slice(turn * width, (turn + 1) * width) for turn in range(rounds)]
    for span, part in zip(spans, halo[rounds:]):
        halo_agg[span, :] = part[...]
    pre = dot(halo_agg[...], first_weight[...])
    sigm = jax.nn.sigmoid(pre)
    halo_slope = (sigm * (1.0 + pre * (1.0 - sigm))).T
    act = pre * sigm
    for span, part in zip(spans, halo[:rounds]):
        halo_hidden[span, :] = (part[...].astype(jnp.float32) + act[span]).astype(jnp.bfloat16)
    second_agg = (inner[...] + dot(halo_bonds[...], halo_hidden[...])).astype(jnp.bfloat16)
    output = hidden[...].astype(jnp.float32) + dot(second_agg, second_weight[...])
    prediction[...] = output.astype(jnp.bfloat16)
    error = (output - targets[...].astype(jnp.float32)) * scale
    error_b = error.astype(jnp.bfloat16)
    agg_cot = dot_last(second_weight[...], error_b).astype(jnp.bfloat16)
    halo_cot = (dot(agg_cot, halo_bonds[...]) * halo_slope).astype(jnp.bfloat16)
    own_cot = ((error.T + dot(agg_cot, bonds[...])) * slope[...]).astype(jnp.bfloat16)
    grad_first = (dot(halo_cot, halo_agg[...]) + dot(own_cot, agg[...])).T
    size = grad_first.shape[0]
    grads[:size, :] = grad_first
    grads[size:, :] = dot_rows(second_agg, error_b)


def mixed(value, even_mask, odd_mask):
    masks = (even_mask, odd_mask)
    pairs = [(source, source ^ masks[source % 2]) for source in range(lax.axis_size("dom"))]
    return lax.ppermute(value, "dom", pairs)


def four_kernel(own, first, second, third, total):
    even = lax.rem(lax.axis_index("dom"), 2) == 0
    own, first, second, third = (
        part[...].astype(jnp.float32) for part in (own, first, second, third)
    )
    summed_up = jnp.where(even, (own + first) + (second + third), (own + second) + (first + third))
    total[...] = summed_up.astype(total.dtype)


def half_kernel(own, near, far, half):
    even = lax.rem(lax.axis_index("dom"), 2) == 0
    mine = jnp.where(even, own[...].astype(jnp.float32), far[...].astype(jnp.float32))
    half[...] = mine + near[...].astype(jnp.float32)


def summed(total):
    size = lax.axis_size("dom")
    wide = [(total.shape, jnp.float32)]
    middle = total.shape[0] // 2
    parts = slice(None, middle), slice(middle, None)
    total = total + swapped(total, 1)
    mask = 2
    while mask < size:
        low = total.astype(jnp.bfloat16)
        if 2 * mask >= size:
            total = low.astype(jnp.float32) + swapped(low, mask).astype(jnp.float32)
        elif mask == 2:
            terms = [
                mixed(low, mask, 2 * mask),
                mixed(low, 2 * mask, mask),
                mixed(low, 3 * mask, 3 * mask),
            ]
            kind = low.dtype if 4 * mask < size else jnp.float32
            (total,) = call(four_kernel, [(low.shape, kind)], low, *terms)
        else:
            near, far = mixed(low, mask, 2 * mask), mixed(low, mask, 3 * mask)
            (half,) = call(half_kernel, wide, low, near, far)
            other = swapped(half, 1)
            if 4 * mask >= size:
                return [half[part] + other[part] for part in parts]
            total = half + other
        mask *= 4
    return [total[part] for part in parts]


def local(
    features, targets, first_weight, second_weight, local_bonds, halo_bonds, tile_mask, send_rows
):
    atoms, wide = features.shape
    rounds, width = send_rows.shape
    low, high = jnp.bfloat16, jnp.float32
    sent = [((width, wide), low)] * rounds
    stacked = pltpu.VMEM((rounds * width, wide), low)
    features, picker = call(
        picker_kernel,
        [((atoms, wide), low), ((rounds * width, atoms), low)],
        features,
        send_rows,
        remain=2,
        scratch=[pltpu.VMEM((rounds, width), jnp.int32), pltpu.SemaphoreType.DMA((2,))],
    )
    picked = call(pick_kernel, sent, picker, features, cost=COST)
    halo = [swapped(part, 2**turn) for turn, part in enumerate(picked)]
    bonds, inner, inner_sent, halo_sent = call(
        inner_kernel,
        [
            ((atoms, atoms), low),
            ((atoms, wide), high),
            ((rounds * width, wide), high),
            ((rounds * width, rounds * width), low),
        ],
        local_bonds,
        tile_mask,
        features,
        halo_bonds,
        picker,
        send_rows,
        scratch=[pltpu.SMEM((rounds, width), jnp.int32), pltpu.SemaphoreType.DMA],
    )
    picked = call(sent_kernel, sent, inner_sent, halo_sent, *halo)
    halo_agg = [swapped(part, 2**turn) for turn, part in enumerate(picked)]
    agg, hidden, slope, inner = call(
        hidden_kernel,
        [
            ((atoms, wide), low),
            ((atoms, wide), low),
            ((wide, atoms), high),
            ((atoms, wide), high),
        ],
        inner,
        halo_bonds,
        first_weight,
        features,
        bonds,
        *halo,
        scratch=[stacked],
    )
    scale = 1.0 / math.sqrt(atoms * lax.axis_size("dom"))
    prediction, grads = call(
        functools.partial(back_kernel, scale),
        [((atoms, wide), low), ((2 * wide, wide), high)],
        inner,
        hidden,
        slope,
        agg,
        bonds,
        halo_bonds,
        targets,
        first_weight,
        second_weight,
        *halo,
        *halo_agg,
        scratch=[stacked, stacked],
    )
    return (prediction, *summed(grads))


def solution(mesh):
    rows = P("dom", None)
    in_specs = (rows, rows, P(), P(), rows, rows, rows, rows)
    out_specs = (rows, P(), P())
    return jax.shard_map(local, mesh=mesh, in_specs=in_specs, out_specs=out_specs, check_vma=False)
```
